32 devices in a mesh: row: 8 (over z, y), col: 4 (over x, core).
Axes of the slice: x: 2, y: 2, z: 4, core: 2. Of those that a mesh axis runs over, the one named last changes fastest.
Arguments:
- struct_disp: float32 [48, 8192], P(None, ('row', 'col')), may hold values from -6 to 6
- target: int32 [8192], P(('row', 'col')), may hold values from 0 to 32767, as said below
- inverse: bfloat16 [32768, 32768], P('row', 'col'), may hold values from -0.09375 to 0.09375
- centre_xyz: float32 [3, 32768], replicated, may hold values from 0 to 1, as said below
- node_xyz: float32 [3, 65536], P(None, ('row', 'col')), may hold values from 0 to 1, as said below
Outputs:
- volume_disp: float32 [48, 65536], P(None, ('row', 'col'))
The draws below stay inside these ranges and needn't reach their ends.
Inputs may be any that keep to these rules, and one draw needn't show every extreme that they name: `target`: centre j is held by the owner of index r * 4 + c with c = j // 8192 and r = (j % 8192) // 1024. The 256 entries of one device name centres of at most 16 entries for any one owner, and one owner receives exactly 16 entries from every device. `centre_xyz`: every centre lies on the boundary of the cube that spans 0.3 to 0.7 in each coordinate. `node_xyz`: every volume node lies outside the cube that spans 0.3 to 0.7 in each coordinate, or on its boundary.
All inputs are finite; a program needn't handle non-finite values.
Results may differ from the reference program's by a relative error of at most 0.0049.
Values may be sent and summed in bfloat16 or wider, within the bound.
A program may use at most 128 MiB of HBM per device.

```python
import math
import jax
import jax.numpy as jnp
from jax import lax

M = 32768
E_DEV = 256
DISP_ROWS = 48
OWNERS = 32
CAP = 16
ENTRIES = 8192
VOL = 65536
BLK = 1024
CB = 8192
N_COL = 4


def draw_target(key, part):
    first_key, second_key, third_key = jax.random.split(jax.random.fold_in(key, 11), 3)
    hot_owner = jax.random.randint(first_key, (), 0, OWNERS)
    sender_keys = jax.random.split(second_key, OWNERS)
    orders = jax.vmap(lambda sender_key: jax.random.permutation(sender_key, OWNERS - 1))(sender_keys)
    others = orders + (orders >= hot_owner).astype(jnp.int32)
    positions = jnp.arange(E_DEV, dtype=jnp.int32)
    rest_pos = jnp.maximum(positions - CAP, 0) % (OWNERS - 1)
    rest_dest = jnp.take_along_axis(others, jnp.broadcast_to(rest_pos[None, :], (OWNERS, E_DEV)), axis=1)
    destination = jnp.where(positions[None, :] < CAP, hot_owner, rest_dest)
    owner_row = destination // N_COL
    owner_col = destination % N_COL
    within = jax.random.randint(third_key, (OWNERS, E_DEV), 0, BLK)
    return (owner_col * CB + owner_row * BLK + within).reshape(-1).astype(jnp.int32)


def face_points(key, how_many, lift_scale):
    face_key, one_key, two_key, lift_key = jax.random.split(key, 4)
    face_ids = jax.random.randint(face_key, (how_many,), 0, 6)
    normal_ids = face_ids // 2
    side_ids = face_ids % 2
    along_one = 0.3 + 0.4 * jax.random.uniform(one_key, (how_many,), jnp.float32)
    along_two = 0.3 + 0.4 * jax.random.uniform(two_key, (how_many,), jnp.float32)
    lift_off = lift_scale * jax.random.uniform(lift_key, (how_many,), jnp.float32)
    plane_at = jnp.where(side_ids == 1, 0.7 + lift_off, 0.3 - lift_off)
    coord_x = jnp.where(normal_ids == 0, plane_at, along_one)
    coord_y = jnp.where(normal_ids == 0, along_one, jnp.where(normal_ids == 1, plane_at, along_two))
    coord_z = jnp.where(normal_ids == 2, plane_at, along_two)
    return jnp.stack([coord_x, coord_y, coord_z], axis=0).astype(jnp.float32)


def draw_centre_xyz(key, part):
    return face_points(jax.random.fold_in(key, 21), M, 0.0)


def draw_node_xyz(key, part):
    support = 2.0 / math.sqrt(M)
    lift_scale = 0.6 * support
    return face_points(jax.random.fold_in(key, 37), VOL, lift_scale)


def with_spikes(entries, own_key, source, target, blocks, factor):
    owner, partner = [(jnp.arange(entries.shape[position]) // (entries.shape[position] // blocks)).reshape([-1 if axis == position else 1 for axis in range(entries.ndim)]) for position in (source, target)]
    chosen = jax.random.permutation(own_key, blocks)[partner]
    strong = (owner == chosen) | (owner == (partner + blocks // 2) % blocks)
    return jnp.where(strong, factor * entries, entries)


def steps_of(rng, dims, shards, smallest, largest):
    def one(axis_at, parts):
        heights = jax.random.uniform(jax.random.fold_in(jax.random.fold_in(rng, 6), axis_at), (parts,), jnp.float32, smallest / len(shards), largest / len(shards))
        return jnp.repeat(jnp.exp(heights), dims[axis_at] // parts).reshape((-1,) + (1,) * (len(dims) - axis_at - 1))

    gain = one(*shards[0])
    for cut in shards[1:]:
        gain = gain * one(*cut)
    return gain


def gaussian(rng, extent, spread, most, pieces=(), held_as=jnp.bfloat16):
    values = jax.random.normal(rng, extent, jnp.float32) * spread
    if len(pieces) > 0:
        values = steps_of(rng, extent, pieces, -0.22, 0.18) * values
    return jnp.clip(values, min=-most, max=most).astype(held_as)


def gaussian_with(key, extent, scale, limit, shards, heavy, kind=jnp.bfloat16):
    values = scale * jax.random.normal(key, extent, jnp.float32)
    if shards:
        values = values * steps_of(key, extent, shards, -0.22, 0.18)
    return jnp.clip(with_spikes(values, jax.random.fold_in(key, 3), *heavy), -limit, limit).astype(kind)


def setup_inputs(seed: int = 0) -> dict:
    arg_keys = jax.random.split(jax.random.key(seed), 6)
    return {
        "struct_disp": gaussian(arg_keys[0], (DISP_ROWS, ENTRIES), 1.0, 6.0, ((1, 32),), jnp.float32),
        "target": draw_target(jax.random.fold_in(arg_keys[5], 71), 0),
        "inverse": gaussian_with(arg_keys[2], (M, M), ENTRIES ** -0.5, 0.09375, ((0, 8), (1, 4)), (1, 0, 8, 2.0)),
        "centre_xyz": draw_centre_xyz(jax.random.fold_in(arg_keys[5], 71), 0),
        "node_xyz": draw_node_xyz(jax.random.fold_in(arg_keys[5], 71), 0),
    }


def wendland_tile(centre_block, node_block):
    radius = 2.0 / math.sqrt(M)
    squared = jnp.zeros((centre_block.shape[1], node_block.shape[1]), jnp.float32)
    for component in range(3):
        difference = centre_block[component][:, None] - node_block[component][None, :]
        squared = squared + difference * difference
    scaled = jnp.sqrt(squared) / radius
    remain = jnp.maximum(1.0 - scaled, 0.0)
    return (remain ** 4 * (4.0 * scaled + 1.0)).astype(jnp.bfloat16)

def reference(struct_disp, target, inverse, centre_xyz, node_xyz):
    centre_disp = jnp.zeros((DISP_ROWS, M), jnp.float32).at[:, target].add(struct_disp)
    disp_bf = centre_disp.astype(jnp.bfloat16)
    coefs = lax.dot_general(disp_bf, inverse, (((1,), (1,)), ((), ())), preferred_element_type=jnp.float32)
    coef_bf = coefs.astype(jnp.bfloat16)
    block_size = math.gcd(VOL, 1024)
    node_blocks = node_xyz.reshape(3, VOL // block_size, block_size).transpose(1, 0, 2)

    def one_block(nodes):
        kernel_tile = wendland_tile(centre_xyz, nodes)
        return jnp.dot(coef_bf, kernel_tile, preferred_element_type=jnp.float32)
    blocks_out = lax.map(one_block, node_blocks)
    return blocks_out.transpose(1, 0, 2).reshape(DISP_ROWS, VOL)
```

```python
import functools
import math

import jax
import jax.numpy as jnp
from jax import lax
from jax.experimental import pallas as pl
from jax.experimental.pallas import tpu as pltpu
from jax.sharding import PartitionSpec as P

M = 32768
RADIUS = 2.0 / math.sqrt(M)
GROUP = 8
CHUNK = 128
BATCH = 32
CELL_BITS = 5


def split_three(values):
    first = lax.reduce_precision(values, 8, 7)
    rest = values - first
    second = lax.reduce_precision(rest, 8, 7)
    third = rest - second
    return jnp.concatenate([first, second, third], axis=0).astype(jnp.bfloat16)


def join_three(stacked):
    rows = stacked.shape[0] // 3
    return stacked[:rows] + stacked[rows : 2 * rows] + stacked[2 * rows :]


def place_key(points):
    centred = points - 0.5
    size = jnp.abs(centred)
    x, y, z = size[0], size[1], size[2]
    on_x = (x >= y) & (x >= z)
    on_y = jnp.logical_not(on_x) & (y >= z)
    axis = jnp.where(on_x, 0, jnp.where(on_y, 1, 2))
    normal = jnp.where(on_x, centred[0], jnp.where(on_y, centred[1], centred[2]))
    u = jnp.where(on_x, points[1], points[0])
    v = jnp.where(on_x | on_y, points[2], points[1])
    cells = 1 << CELL_BITS
    iu = jnp.clip(jnp.floor((u - 0.3) * (cells / 0.4)), 0, cells - 1).astype(jnp.int32)
    iv = jnp.clip(jnp.floor((v - 0.3) * (cells / 0.4)), 0, cells - 1).astype(jnp.int32)
    code = axis * 2 + (normal > 0).astype(jnp.int32)
    for bit in reversed(range(CELL_BITS)):
        code = code * 4 + ((iu >> bit) & 1) * 2 + ((iv >> bit) & 1)
    return code


def ranks(points):
    count = points.shape[1]
    key = place_key(points) * count + jnp.arange(count, dtype=jnp.int32)
    return jnp.sum((key[:, None] < key[None, :]).astype(jnp.int32), axis=0)


def one_hot(ids, first, count):
    wanted = first + jnp.arange(count, dtype=jnp.int32)
    return (wanted[:, None] == ids[None, :]).astype(jnp.bfloat16)


def times_rows(left, right):
    return lax.dot_general(
        left, right, (((1,), (1,)), ((), ())), preferred_element_type=jnp.float32
    )


def volume_kernel(chunks, groups, counts, lists, centres, nodes, coefs, out, spread):
    total = groups + 1

    def spread_one(g, carry):
        rows = pl.ds(pl.multiple_of(g * GROUP, GROUP), GROUP)
        block = nodes[rows, :]
        for d in range(3):
            spread[d, rows, :] = jnp.broadcast_to(block[:, d : d + 1], (GROUP, 128))
        return carry

    lax.fori_loop(0, total, spread_one, 0)
    out[...] = jnp.zeros_like(out)

    def one_chunk(c, carry):
        columns = pl.ds(pl.multiple_of(c * CHUNK, CHUNK), CHUNK)
        here = [centres[d : d + 1, columns] for d in range(3)]
        coef = coefs[:, columns]

        def one_batch(b, inner):
            tiles = []
            starts = []
            for g in range(BATCH):
                start = pl.multiple_of(lists[c, b * BATCH + g] * GROUP, GROUP)
                starts.append(start)
                squared = None
                for d in range(3):
                    difference = spread[d, pl.ds(start, GROUP), :] - here[d]
                    term = difference * difference
                    squared = term if squared is None else squared + term
                scaled = jnp.sqrt(squared)
                remain = jnp.maximum(1.0 - scaled, 0.0)
                remain = remain * remain
                remain = remain * remain
                tiles.append(remain * (4.0 * scaled + 1.0))
            phi = jnp.concatenate(tiles, axis=0).astype(jnp.bfloat16)
            product = times_rows(phi, coef)
            for g in range(BATCH):
                rows = pl.ds(starts[g], GROUP)
                out[rows, :] += product[g * GROUP : (g + 1) * GROUP]
            return inner

        batches = (counts[c] + (BATCH - 1)) // BATCH
        return lax.fori_loop(0, batches, one_batch, carry)

    lax.fori_loop(0, chunks, one_chunk, 0)


def volume(coefs, centres, nodes):
    centre_count = centres.shape[1]
    node_count = nodes.shape[1]
    chunks = centre_count // CHUNK
    groups = node_count // GROUP
    centre_boxes = centres.reshape(3, chunks, CHUNK)
    node_boxes = nodes.reshape(3, groups, GROUP)
    gap = jnp.maximum(
        jnp.min(centre_boxes, axis=2)[:, :, None] - jnp.max(node_boxes, axis=2)[:, None, :],
        jnp.min(node_boxes, axis=2)[:, None, :] - jnp.max(centre_boxes, axis=2)[:, :, None],
    )
    gap = jnp.maximum(gap, 0.0)
    near = jnp.sum(gap * gap, axis=0) <= RADIUS * RADIUS * 1.001
    near_f = near.astype(jnp.bfloat16)
    earlier = (jnp.arange(groups)[:, None] < jnp.arange(groups)[None, :]).astype(jnp.bfloat16)
    place = lax.dot_general(
        near_f, earlier, (((1,), (0,)), ((), ())), preferred_element_type=jnp.float32
    ).astype(jnp.int32)
    place = jnp.where(near, place, -1)
    counts = jnp.sum(near.astype(jnp.int32), axis=1)
    slots = -(-groups // BATCH) * BATCH
    hit = place[:, None, :] == jnp.arange(slots, dtype=jnp.int32)[None, :, None]
    lists = groups + jnp.sum(
        jnp.where(hit, jnp.arange(groups, dtype=jnp.int32)[None, None, :] - groups, 0), axis=2
    )
    scale = 1.0 / RADIUS
    far = jnp.full((GROUP, 3), 1e4, jnp.float32)
    node_rows = jnp.concatenate([nodes.T * scale, far], axis=0)
    smem = pl.BlockSpec(memory_space=pltpu.SMEM)
    vmem = pl.BlockSpec(memory_space=pltpu.VMEM)
    result = pl.pallas_call(
        functools.partial(volume_kernel, chunks, groups),
        out_shape=jax.ShapeDtypeStruct((node_count + GROUP, coefs.shape[0]), jnp.float32),
        in_specs=[smem, smem, vmem, vmem, vmem],
        out_specs=vmem,
        scratch_shapes=[pltpu.VMEM((3, node_count + GROUP, 128), jnp.float32)],
        compiler_params=pltpu.CompilerParams(vmem_limit_bytes=40 * 1024 * 1024),
        name="volume",
    )(counts, lists, centres * scale, node_rows, coefs)
    return result[:node_count]


def per_device(struct_disp, target, inverse, centre_xyz, node_xyz):
    row_count = lax.axis_size("row")
    col_count = lax.axis_size("col")
    owner_count = row_count * col_count
    row_at = lax.axis_index("row")
    col_at = lax.axis_index("col")
    row_block, col_block = inverse.shape
    owner_block = row_block // col_count
    own_piece = row_block // col_count
    disp_rows, entries = struct_disp.shape

    slot_cap = max(2, 2 * entries // owner_count)
    owner_ids = target % col_block // owner_block * col_count + target // col_block
    offsets = target % owner_block
    at = jnp.arange(entries, dtype=jnp.int32)
    same = (owner_ids[:, None] == owner_ids[None, :]) & (at[:, None] < at[None, :])
    ranking = jnp.sum(same.astype(jnp.int32), axis=0)
    slot_ids = owner_ids * slot_cap + ranking
    pick = one_hot(slot_ids, 0, owner_count * slot_cap)
    outgoing = jnp.concatenate([struct_disp, offsets.astype(jnp.float32)[None, :] + 1.0], axis=0)
    sent = times_rows(pick, split_three(outgoing))
    width = disp_rows + 1
    sent = sent[:, :width] + sent[:, width : 2 * width] + sent[:, 2 * width :]
    received = lax.all_to_all(sent, ("row", "col"), split_axis=0, concat_axis=0, tiled=True)
    recv_offsets = received[:, disp_rows].astype(jnp.int32) - 1
    spots = one_hot(recv_offsets, 0, owner_block)
    centre_disp = join_three(times_rows(split_three(received[:, :disp_rows].T), spots))
    disp_bf = centre_disp.astype(jnp.bfloat16)
    disp_block = lax.all_gather(disp_bf, "row", axis=1, tiled=True)

    mine = lax.dynamic_slice_in_dim(centre_xyz, row_at * row_block, row_block, 1)
    order = one_hot(ranks(mine), col_at * own_piece, own_piece)
    placed_xyz = join_three(times_rows(split_three(mine), order))
    centres = lax.all_gather(placed_xyz, ("row", "col"), axis=1, tiled=True)
    node_order = one_hot(ranks(node_xyz), 0, node_xyz.shape[1])
    nodes = join_three(times_rows(split_three(node_xyz), node_order))

    partial_value = times_rows(disp_block, inverse)
    coef_bf = lax.psum(partial_value, "col").astype(jnp.bfloat16)
    placed_coefs = times_rows(coef_bf, order).astype(jnp.bfloat16)
    coefs = lax.all_gather(placed_coefs, ("row", "col"), axis=1, tiled=True)
    result = volume(coefs, centres, nodes)
    back = lax.dot_general(
        split_three(result.T), node_order, (((1,), (0,)), ((), ())), preferred_element_type=jnp.float32
    )
    return join_three(back)


def solution(mesh):
    placed = (
        P(None, ("row", "col")),
        P(("row", "col")),
        P("row", "col"),
        P(),
        P(None, ("row", "col")),
    )
    return jax.shard_map(
        per_device, mesh=mesh, in_specs=placed, out_specs=P(None, ("row", "col")), check_vma=False
    )
```

```python
import functools
import math

import jax
import jax.numpy as jnp
from jax import lax
from jax.experimental import pallas as pl
from jax.experimental.pallas import tpu as pltpu
from jax.sharding import PartitionSpec as P

M = 32768
RADIUS = 2.0 / math.sqrt(M)
GROUP = 8
CHUNK = 128
BATCH = 32
SUB = 16
CELL_BITS = 5


def split_three(values):
    first = lax.reduce_precision(values, 8, 7)
    rest = values - first
    second = lax.reduce_precision(rest, 8, 7)
    third = rest - second
    return jnp.concatenate([first, second, third], axis=0).astype(jnp.bfloat16)


def join_three(stacked):
    rows = stacked.shape[0] // 3
    return stacked[:rows] + stacked[rows : 2 * rows] + stacked[2 * rows :]


def place_key(points):
    centred = points - 0.5
    size = jnp.abs(centred)
    x, y, z = size[0], size[1], size[2]
    on_x = (x >= y) & (x >= z)
    on_y = jnp.logical_not(on_x) & (y >= z)
    axis = jnp.where(on_x, 0, jnp.where(on_y, 1, 2))
    normal = jnp.where(on_x, centred[0], jnp.where(on_y, centred[1], centred[2]))
    u = jnp.where(on_x, points[1], points[0])
    v = jnp.where(on_x | on_y, points[2], points[1])
    cells = 1 << CELL_BITS
    iu = jnp.clip(jnp.floor((u - 0.3) * (cells / 0.4)), 0, cells - 1).astype(jnp.int32)
    iv = jnp.clip(jnp.floor((v - 0.3) * (cells / 0.4)), 0, cells - 1).astype(jnp.int32)
    code = axis * 2 + (normal > 0).astype(jnp.int32)
    for bit in reversed(range(CELL_BITS)):
        code = code * 4 + ((iu >> bit) & 1) * 2 + ((iv >> bit) & 1)
    return code


def ranks(points):
    count = points.shape[1]
    key = place_key(points) * count + jnp.arange(count, dtype=jnp.int32)
    return jnp.sum((key[:, None] < key[None, :]).astype(jnp.int32), axis=0)


def one_hot(ids, first, count):
    wanted = first + jnp.arange(count, dtype=jnp.int32)
    return (wanted[:, None] == ids[None, :]).astype(jnp.bfloat16)


def times_rows(left, right):
    return lax.dot_general(
        left, right, (((1,), (1,)), ((), ())), preferred_element_type=jnp.float32
    )


def gather_kernel(sizes, plans, pair_up, block, out, send_sem, recv_sem):
    z_size, y_size, x_size = sizes
    row_at = lax.axis_index("row")
    col_at = lax.axis_index("col")
    at = {
        "z": lax.div(row_at, y_size),
        "y": lax.rem(row_at, y_size),
        "x": lax.div(col_at, 2),
        "k": lax.rem(col_at, 2),
    }
    lengths = {"z": z_size, "y": y_size, "x": x_size, "k": 2}
    used = ["z", "y", "x"] if pair_up else ["z", "y"]

    def moved(axis, step):
        place = dict(at)
        place[axis] = lax.rem(at[axis] + step, lengths[axis])
        return place

    def device(place):
        return (place["z"] * y_size + place["y"], place["x"] * 2 + place["k"])

    partners = [(axis, step) for axis in used for step in range(1, lengths[axis])]
    if pair_up:
        partners.append(("k", 1))
    barrier = pltpu.get_barrier_semaphore()
    for axis, step in partners:
        pl.semaphore_signal(
            barrier, inc=1, device_id=device(moved(axis, step)), device_id_type=pl.DeviceIdType.MESH
        )
    pl.semaphore_wait(barrier, len(partners))

    def slab(place, columns):
        index = tuple(slice(None) if place[axis] is None else place[axis] for axis in used)
        if pair_up:
            index = index + (at["k"],)
        return out.at[index + (slice(None), columns)]

    out[tuple(at[axis] for axis in used) + ((at["k"],) if pair_up else ())] = block[...]
    unsent = []
    unmet = []
    count = 0

    def push(place, columns, axis, step):
        nonlocal count
        region = slab(place, columns)
        copy = pltpu.make_async_remote_copy(
            src_ref=region,
            dst_ref=region,
            send_sem=send_sem.at[count],
            recv_sem=recv_sem.at[count],
            device_id=device(moved(axis, step)),
            device_id_type=pl.DeviceIdType.MESH,
        )
        copy.start()
        count += 1
        unsent.append(copy)
        return copy

    width = out.shape[-1] // len(plans)
    parts = [slice(i * width, (i + 1) * width) for i in range(len(plans))]
    held = [dict(at) for _ in plans]
    for stage in range(len(used)):
        copies = []
        for part, plan in enumerate(plans):
            axis = plan[stage]
            for step in range(1, lengths[axis]):
                copies.append((part, axis, step, push(held[part], parts[part], axis, step)))
        if stage == 0 and pair_up:
            for part in range(len(plans)):
                unmet.append(push(held[part], parts[part], "k", 1))
        for part, axis, step, copy in copies:
            copy.wait_recv()
            if pair_up:
                place = dict(held[part])
                place[axis] = lax.rem(at[axis] - step + lengths[axis], lengths[axis])
                unmet.append(push(place, parts[part], "k", 1))
        for part, plan in enumerate(plans):
            held[part][plan[stage]] = None
    for copy in unmet:
        copy.wait_recv()
    for copy in unsent:
        copy.wait_send()


def gather(block, row_count, col_count, plans, pair_up, collective_id):
    y_size = 2 if row_count % 2 == 0 else 1
    sizes = (row_count // y_size, y_size, col_count // 2)
    leading = (*sizes, 2) if pair_up else sizes[:2]
    stages = 3 if pair_up else 2
    hops = sum(sizes[:stages]) - stages
    copies = len(plans) * (2 * hops + 1)
    vmem = pl.BlockSpec(memory_space=pltpu.VMEM)
    out = pl.pallas_call(
        functools.partial(gather_kernel, sizes, plans, pair_up),
        out_shape=jax.ShapeDtypeStruct((*leading, *block.shape), block.dtype),
        in_specs=[vmem],
        out_specs=vmem,
        scratch_shapes=[pltpu.SemaphoreType.DMA((copies,)), pltpu.SemaphoreType.DMA((copies,))],
        compiler_params=pltpu.CompilerParams(
            collective_id=collective_id,
            has_side_effects=True,
            vmem_limit_bytes=24 * 1024 * 1024,
        ),
        name="gather",
    )(block)
    return out.reshape(math.prod(leading), *block.shape)


def compact_kernel(place_ref, lists):
    place = place_ref[...]
    width = place.shape[1]
    group = lax.broadcasted_iota(jnp.int32, place.shape, 1)
    value = jnp.where(place >= 0, (group - place) * 2 * width + group, -1)
    step = 1
    while step < width:
        shifted = pltpu.roll(value, width - step, 1)
        bit = step * 2 * width
        arrives = (shifted >= 0) & ((shifted & bit) != 0)
        stays = (value >= 0) & ((value & bit) == 0)
        value = jnp.where(arrives, shifted, jnp.where(stays, value, -1))
        step *= 2
    lists[...] = jnp.where(value >= 0, value & (2 * width - 1), width)


def volume_kernel(groups, counts, lists, centres, nodes, coefs, out, spread, items):
    total = groups + 1
    chunks = counts.shape[0]
    per_block = coefs.shape[2] // CHUNK
    batches = groups // BATCH

    def list_chunk(c, count):
        def list_one(b, n):
            items[n] = c * batches + b
            return n + 1

        return lax.fori_loop(0, (counts[c] + (BATCH - 1)) // BATCH, list_one, count)

    item_count = lax.fori_loop(0, chunks, list_chunk, 0)

    def spread_one(g, carry):
        rows = pl.ds(pl.multiple_of(g * GROUP, GROUP), GROUP)
        block = nodes[rows, :]
        for d in range(3):
            spread[d, rows, :] = jnp.broadcast_to(block[:, d : d + 1], (GROUP, 128))
        return carry

    lax.fori_loop(0, total, spread_one, 0)
    out[...] = jnp.zeros_like(out)

    def evaluate(item, live):
        c = lax.div(item, batches)
        b = lax.rem(item, batches)
        columns = pl.ds(pl.multiple_of(c * CHUNK, CHUNK), CHUNK)
        here = [jnp.broadcast_to(centres[d : d + 1, columns], (GROUP, CHUNK)) for d in range(3)]
        within = pl.ds(pl.multiple_of(lax.rem(c, per_block) * CHUNK, CHUNK), CHUNK)
        coef = coefs[lax.div(c, per_block), :, within]
        tiles = []
        starts = []
        for g in range(BATCH):
            group = lists[c, b * BATCH + g]
            if live is not None:
                group = jnp.where(live, group, groups)
            start = pl.multiple_of(group * GROUP, GROUP)
            starts.append(start)
            squared = None
            for d in range(3):
                difference = spread[d, pl.ds(start, GROUP), :] - here[d]
                term = difference * difference
                squared = term if squared is None else squared + term
            squared = jnp.maximum(squared, 1e-30)
            scaled = squared * lax.rsqrt(squared)
            remain = jnp.maximum(1.0 - scaled, 0.0)
            remain = remain * remain
            remain = remain * remain
            tiles.append(remain * (4.0 * scaled + 1.0))
        phi = jnp.concatenate(tiles, axis=0).astype(jnp.bfloat16)
        return starts, times_rows(phi, coef)

    def add_up(starts, product):
        for g in range(BATCH):
            rows = pl.ds(starts[g], GROUP)
            out[rows, :] += product[g * GROUP : (g + 1) * GROUP]

    def two_items(n, carry):
        second = 2 * n + 1
        live = second < item_count
        first_starts, first_product = evaluate(items[2 * n], None)
        second_starts, second_product = evaluate(items[jnp.minimum(second, item_count - 1)], live)
        add_up(first_starts, first_product)
        add_up(second_starts, second_product)
        return carry

    lax.fori_loop(0, (item_count + 1) // 2, two_items, 0)


def volume_lists(centres, nodes):
    centre_count = centres.shape[1]
    chunks = centre_count // CHUNK
    groups = nodes.shape[1] // GROUP
    centre_boxes = centres.reshape(3, centre_count // SUB, SUB)
    node_boxes = nodes.reshape(3, groups, GROUP)
    gap = jnp.maximum(
        jnp.min(centre_boxes, axis=2)[:, :, None] - jnp.max(node_boxes, axis=2)[:, None, :],
        jnp.min(node_boxes, axis=2)[:, None, :] - jnp.max(centre_boxes, axis=2)[:, :, None],
    )
    gap = jnp.maximum(gap, 0.0)
    least = jnp.min(jnp.sum(gap * gap, axis=0).reshape(chunks, CHUNK // SUB, groups), axis=1)
    near = least <= RADIUS * RADIUS * 1.001
    earlier = (jnp.arange(groups)[:, None] < jnp.arange(groups)[None, :]).astype(jnp.bfloat16)
    place = lax.dot_general(
        near.astype(jnp.bfloat16), earlier, (((1,), (0,)), ((), ())), preferred_element_type=jnp.float32
    ).astype(jnp.int32)
    counts = jnp.sum(near.astype(jnp.int32), axis=1)
    lists = pl.pallas_call(
        compact_kernel,
        out_shape=jax.ShapeDtypeStruct((chunks, groups), jnp.int32),
        name="compact",
    )(jnp.where(near, place, -1))
    return counts, lists


def volume(coefs, centres, nodes):
    node_count = nodes.shape[1]
    groups = node_count // GROUP
    counts, lists = volume_lists(centres, nodes)
    scale = 1.0 / RADIUS
    far = jnp.full((GROUP, 3), 1e4, jnp.float32)
    node_rows = jnp.concatenate([nodes.T * scale, far], axis=0)
    smem = pl.BlockSpec(memory_space=pltpu.SMEM)
    vmem = pl.BlockSpec(memory_space=pltpu.VMEM)
    result = pl.pallas_call(
        functools.partial(volume_kernel, groups),
        out_shape=jax.ShapeDtypeStruct((node_count + GROUP, coefs.shape[1]), jnp.float32),
        in_specs=[smem, smem, vmem, vmem, vmem],
        out_specs=vmem,
        scratch_shapes=[
            pltpu.VMEM((3, node_count + GROUP, 128), jnp.float32),
            pltpu.SMEM((counts.shape[0] * (groups // BATCH),), jnp.int32),
        ],
        compiler_params=pltpu.CompilerParams(vmem_limit_bytes=40 * 1024 * 1024),
        name="volume",
    )(counts, lists, centres * scale, node_rows, coefs)
    return result[:node_count]


def per_device(struct_disp, target, inverse, centre_xyz, node_xyz):
    row_count = lax.axis_size("row")
    col_count = lax.axis_size("col")
    owner_count = row_count * col_count
    row_at = lax.axis_index("row")
    col_at = lax.axis_index("col")
    row_block, col_block = inverse.shape
    owner_block = row_block // col_count
    own_piece = row_block // col_count
    disp_rows, entries = struct_disp.shape

    slot_cap = max(2, 2 * entries // owner_count)
    owner_ids = target % col_block // owner_block * col_count + target // col_block
    offsets = target % owner_block
    at = jnp.arange(entries, dtype=jnp.int32)
    same = (owner_ids[:, None] == owner_ids[None, :]) & (at[:, None] < at[None, :])
    ranking = jnp.sum(same.astype(jnp.int32), axis=0)
    slot_ids = owner_ids * slot_cap + ranking
    pick = one_hot(slot_ids, 0, owner_count * slot_cap)
    outgoing = jnp.concatenate([struct_disp, offsets.astype(jnp.float32)[None, :] + 1.0], axis=0)
    sent = times_rows(pick, split_three(outgoing))
    width = disp_rows + 1
    sent = sent[:, :width] + sent[:, width : 2 * width] + sent[:, 2 * width :]
    received = lax.all_to_all(sent, ("row", "col"), split_axis=0, concat_axis=0, tiled=True)
    recv_offsets = received[:, disp_rows].astype(jnp.int32) - 1
    spots = one_hot(recv_offsets, 0, owner_block)
    centre_disp = join_three(times_rows(split_three(received[:, :disp_rows].T), spots))
    disp_bf = centre_disp.astype(jnp.bfloat16)
    halves = (("z", "y"), ("y", "z"))
    disp_block = gather(disp_bf, row_count, col_count, halves, False, 1)
    disp_block = disp_block.transpose(1, 0, 2).reshape(disp_rows, col_block)

    mine = lax.dynamic_slice_in_dim(centre_xyz, row_at * row_block, row_block, 1)
    order = one_hot(ranks(mine), col_at * own_piece, own_piece)
    placed_xyz = join_three(times_rows(split_three(mine), order))
    placed_xyz = jnp.concatenate([placed_xyz, jnp.zeros((5, own_piece), jnp.float32)], axis=0)
    centres = gather(placed_xyz, row_count, col_count, (("x", "y", "z"),), True, 2)
    centres = centres[:, :3].transpose(1, 0, 2).reshape(3, centre_xyz.shape[1])
    node_order = one_hot(ranks(node_xyz), 0, node_xyz.shape[1])
    nodes = join_three(times_rows(split_three(node_xyz), node_order))

    partial_value = times_rows(disp_block, inverse)
    coef_bf = lax.psum(partial_value, "col").astype(jnp.bfloat16)
    placed_coefs = times_rows(coef_bf, order).astype(jnp.bfloat16)
    orders = (("x", "y", "z"), ("z", "x", "y"))
    coefs = gather(placed_coefs, row_count, col_count, orders, True, 3)
    result = volume(coefs, centres, nodes)
    back = lax.dot_general(
        split_three(result.T), node_order, (((1,), (0,)), ((), ())), preferred_element_type=jnp.float32
    )
    return join_three(back)


def solution(mesh):
    placed = (
        P(None, ("row", "col")),
        P(("row", "col")),
        P("row", "col"),
        P(),
        P(None, ("row", "col")),
    )
    return jax.shard_map(
        per_device, mesh=mesh, in_specs=placed, out_specs=P(None, ("row", "col")), check_vma=False
    )
```

```python
import functools
import math

import jax
import jax.numpy as jnp
from jax import lax
from jax.experimental import pallas as pl
from jax.experimental.pallas import tpu as pltpu
from jax.sharding import PartitionSpec as P

M = 32768
RADIUS = 2.0 / math.sqrt(M)
GROUP = 8
CHUNK = 128
BATCH = 24
TOGETHER = 4
SUB = 16
LEVELS = 1024


def split_three(values):
    first = lax.reduce_precision(values, 8, 7)
    rest = values - first
    second = lax.reduce_precision(rest, 8, 7)
    third = rest - second
    return jnp.concatenate([first, second, third], axis=0).astype(jnp.bfloat16)


def join_three(stacked):
    rows = stacked.shape[0] // 3
    return stacked[:rows] + stacked[rows : 2 * rows] + stacked[2 * rows :]


def place_key(points, strips):
    centred = points - 0.5
    size = jnp.abs(centred)
    x, y, z = size[0], size[1], size[2]
    on_x = (x >= y) & (x >= z)
    on_y = jnp.logical_not(on_x) & (y >= z)
    axis = jnp.where(on_x, 0, jnp.where(on_y, 1, 2))
    normal = jnp.where(on_x, centred[0], jnp.where(on_y, centred[1], centred[2]))
    u = jnp.where(on_x, points[1], points[0])
    v = jnp.where(on_x | on_y, points[2], points[1])
    strip = jnp.clip(jnp.floor((u - 0.3) * (strips / 0.4)), 0, strips - 1).astype(jnp.int32)
    along = jnp.clip(jnp.floor((v - 0.3) * (LEVELS / 0.4)), 0, LEVELS - 1).astype(jnp.int32)
    along = jnp.where(strip % 2 == 1, LEVELS - 1 - along, along)
    face = axis * 2 + (normal > 0).astype(jnp.int32)
    return (face * strips + strip) * LEVELS + along


def even_strips(count, run):
    return max(2, 2 * round(math.sqrt(count / 6 / run) / 2))


def ranks(points, run):
    count = points.shape[1]
    key = place_key(points, even_strips(count, run)) * count + jnp.arange(count, dtype=jnp.int32)
    return jnp.sum((key[:, None] < key[None, :]).astype(jnp.int32), axis=0)


def one_hot(ids, first, count):
    wanted = first + jnp.arange(count, dtype=jnp.int32)
    return (wanted[:, None] == ids[None, :]).astype(jnp.bfloat16)


def times_rows(left, right):
    return lax.dot_general(
        left, right, (((1,), (1,)), ((), ())), preferred_element_type=jnp.float32
    )


def gather_kernel(sizes, plans, pair_up, block, out, send_sem, recv_sem):
    z_size, y_size, x_size = sizes
    row_at = lax.axis_index("row")
    col_at = lax.axis_index("col")
    at = {
        "z": lax.div(row_at, y_size),
        "y": lax.rem(row_at, y_size),
        "x": lax.div(col_at, 2),
        "k": lax.rem(col_at, 2),
    }
    lengths = {"z": z_size, "y": y_size, "x": x_size, "k": 2}
    used = ["z", "y", "x"] if pair_up else ["z", "y"]

    def moved(axis, step):
        place = dict(at)
        place[axis] = lax.rem(at[axis] + step, lengths[axis])
        return place

    def device(place):
        return (place["z"] * y_size + place["y"], place["x"] * 2 + place["k"])

    partners = [(axis, step) for axis in used for step in range(1, lengths[axis])]
    if pair_up:
        partners.append(("k", 1))
    barrier = pltpu.get_barrier_semaphore()
    for axis, step in partners:
        pl.semaphore_signal(
            barrier, inc=1, device_id=device(moved(axis, step)), device_id_type=pl.DeviceIdType.MESH
        )
    pl.semaphore_wait(barrier, len(partners))

    def slab(place, columns):
        index = tuple(slice(None) if place[axis] is None else place[axis] for axis in used)
        if pair_up:
            index = index + (at["k"],)
        return out.at[index + (slice(None), columns)]

    out[tuple(at[axis] for axis in used) + ((at["k"],) if pair_up else ())] = block[...]
    unsent = []
    unmet = []
    count = 0

    def push(place, columns, axis, step):
        nonlocal count
        region = slab(place, columns)
        copy = pltpu.make_async_remote_copy(
            src_ref=region,
            dst_ref=region,
            send_sem=send_sem.at[count],
            recv_sem=recv_sem.at[count],
            device_id=device(moved(axis, step)),
            device_id_type=pl.DeviceIdType.MESH,
        )
        copy.start()
        count += 1
        unsent.append(copy)
        return copy

    parts = [columns for _, columns in plans]
    plans = [plan for plan, _ in plans]
    held = [dict(at) for _ in plans]
    for stage in range(len(used)):
        copies = []
        for part, plan in enumerate(plans):
            axis = plan[stage]
            for step in range(1, lengths[axis]):
                copies.append((part, axis, step, push(held[part], parts[part], axis, step)))
        if stage == 0 and pair_up:
            for part in range(len(plans)):
                unmet.append(push(held[part], parts[part], "k", 1))
        for part, axis, step, copy in copies:
            copy.wait_recv()
            if pair_up:
                place = dict(held[part])
                place[axis] = lax.rem(at[axis] - step + lengths[axis], lengths[axis])
                unmet.append(push(place, parts[part], "k", 1))
        for part, plan in enumerate(plans):
            held[part][plan[stage]] = None
    for copy in unmet:
        copy.wait_recv()
    for copy in unsent:
        copy.wait_send()


def gather(block, row_count, col_count, orders, shares, pair_up, collective_id):
    units = block.shape[1] // 128
    if units % sum(shares) != 0:
        orders, shares = (orders[-2:], (1, 1)) if units % 2 == 0 else (orders[-1:], (1,))
    share = block.shape[1] // sum(shares)
    edges = [sum(shares[:i]) * share for i in range(len(shares) + 1)]
    plans = [(order, slice(edges[i], edges[i + 1])) for i, order in enumerate(orders)]
    y_size = 2 if row_count % 2 == 0 else 1
    sizes = (row_count // y_size, y_size, col_count // 2)
    leading = (*sizes, 2) if pair_up else sizes[:2]
    stages = 3 if pair_up else 2
    hops = sum(sizes[:stages]) - stages
    copies = len(plans) * (2 * hops + 1)
    vmem = pl.BlockSpec(memory_space=pltpu.VMEM)
    out = pl.pallas_call(
        functools.partial(gather_kernel, sizes, plans, pair_up),
        out_shape=jax.ShapeDtypeStruct((*leading, *block.shape), block.dtype),
        in_specs=[vmem],
        out_specs=vmem,
        scratch_shapes=[pltpu.SemaphoreType.DMA((copies,)), pltpu.SemaphoreType.DMA((copies,))],
        compiler_params=pltpu.CompilerParams(
            collective_id=collective_id,
            has_side_effects=True,
            vmem_limit_bytes=24 * 1024 * 1024,
        ),
        name="gather",
    )(block)
    return out.reshape(math.prod(leading), *block.shape)


def compact_kernel(place_ref, lists):
    place = place_ref[...]
    width = place.shape[1]
    group = lax.broadcasted_iota(jnp.int32, place.shape, 1)
    value = jnp.where(place >= 0, (group - place) * 2 * width + group, -1)
    step = 1
    while step < width:
        shifted = pltpu.roll(value, width - step, 1)
        bit = step * 2 * width
        arrives = (shifted >= 0) & ((shifted & bit) != 0)
        stays = (value >= 0) & ((value & bit) == 0)
        value = jnp.where(arrives, shifted, jnp.where(stays, value, -1))
        step *= 2
    lists[...] = jnp.where(value >= 0, value & (2 * width - 1), width)


def volume_kernel(groups, counts, lists, centres, nodes, coefs, out, spread, items):
    total = groups + 1
    chunks = counts.shape[0]
    per_block = coefs.shape[2] // CHUNK
    batches = lists.shape[1] // BATCH

    def list_chunk(c, count):
        def list_one(b, n):
            items[n] = c * batches + b
            return n + 1

        return lax.fori_loop(0, (counts[c] + (BATCH - 1)) // BATCH, list_one, count)

    item_count = lax.fori_loop(0, chunks, list_chunk, 0)
    for n in range(TOGETHER - 1):
        items[item_count + n] = chunks * batches

    def spread_one(g, carry):
        rows = pl.ds(pl.multiple_of(g * GROUP, GROUP), GROUP)
        block = nodes[rows, :]
        for d in range(3):
            spread[d, rows, :] = jnp.broadcast_to(block[:, d : d + 1], (GROUP, 128))
        return carry

    lax.fori_loop(0, total, spread_one, 0)
    out[...] = jnp.zeros_like(out)

    def evaluate(item):
        row = lax.div(item, batches)
        first = lax.rem(item, batches) * BATCH
        c = jnp.minimum(row, chunks - 1)
        columns = pl.ds(pl.multiple_of(c * CHUNK, CHUNK), CHUNK)
        here = [jnp.broadcast_to(centres[d : d + 1, columns], (GROUP, CHUNK)) for d in range(3)]
        within = pl.ds(pl.multiple_of(lax.rem(c, per_block) * CHUNK, CHUNK), CHUNK)
        coef = coefs[lax.div(c, per_block), :, within]
        tiles = []
        starts = []
        for g in range(BATCH):
            start = pl.multiple_of(lists[row, first + g] * GROUP, GROUP)
            starts.append(start)
            squared = None
            for d in range(3):
                difference = spread[d, pl.ds(start, GROUP), :] - here[d]
                term = difference * difference
                squared = term if squared is None else squared + term
            squared = jnp.maximum(squared, 1e-30)
            scaled = squared * lax.rsqrt(squared)
            remain = jnp.maximum(1.0 - scaled, 0.0)
            remain = remain * remain
            remain = remain * remain
            tiles.append(remain * (4.0 * scaled + 1.0))
        phi = jnp.concatenate(tiles, axis=0).astype(jnp.bfloat16)
        return starts, times_rows(phi, coef)

    def add_up(starts, product):
        for g in range(BATCH):
            rows = pl.ds(starts[g], GROUP)
            out[rows, :] += product[g * GROUP : (g + 1) * GROUP]

    def some_items(n, carry):
        results = [evaluate(items[TOGETHER * n + i]) for i in range(TOGETHER)]
        for starts, product in results:
            add_up(starts, product)
        return carry

    lax.fori_loop(0, lax.div(item_count + (TOGETHER - 1), TOGETHER), some_items, 0)


def volume_lists(centres, nodes):
    centre_count = centres.shape[1]
    chunks = centre_count // CHUNK
    groups = nodes.shape[1] // GROUP
    centre_boxes = centres.reshape(3, centre_count // SUB, SUB)
    node_boxes = nodes.reshape(3, groups, GROUP)
    gap = jnp.maximum(
        jnp.min(centre_boxes, axis=2)[:, :, None] - jnp.max(node_boxes, axis=2)[:, None, :],
        jnp.min(node_boxes, axis=2)[:, None, :] - jnp.max(centre_boxes, axis=2)[:, :, None],
    )
    gap = jnp.maximum(gap, 0.0)
    least = jnp.min(jnp.sum(gap * gap, axis=0).reshape(chunks, CHUNK // SUB, groups), axis=1)
    near = least <= RADIUS * RADIUS * 1.001
    earlier = (jnp.arange(groups)[:, None] < jnp.arange(groups)[None, :]).astype(jnp.bfloat16)
    place = lax.dot_general(
        near.astype(jnp.bfloat16), earlier, (((1,), (0,)), ((), ())), preferred_element_type=jnp.float32
    ).astype(jnp.int32)
    counts = jnp.sum(near.astype(jnp.int32), axis=1)
    lists = pl.pallas_call(
        compact_kernel,
        out_shape=jax.ShapeDtypeStruct((chunks, groups), jnp.int32),
        name="compact",
    )(jnp.where(near, place, -1))
    spare = -(-groups // BATCH) * BATCH - groups
    return counts, jnp.pad(lists, ((0, 1), (0, spare)), constant_values=groups)


def volume(coefs, centres, nodes):
    node_count = nodes.shape[1]
    groups = node_count // GROUP
    counts, lists = volume_lists(centres, nodes)
    scale = 1.0 / RADIUS
    far = jnp.full((GROUP, 3), 1e4, jnp.float32)
    node_rows = jnp.concatenate([nodes.T * scale, far], axis=0)
    smem = pl.BlockSpec(memory_space=pltpu.SMEM)
    vmem = pl.BlockSpec(memory_space=pltpu.VMEM)
    result = pl.pallas_call(
        functools.partial(volume_kernel, groups),
        out_shape=jax.ShapeDtypeStruct((node_count + GROUP, coefs.shape[1]), jnp.float32),
        in_specs=[smem, smem, vmem, vmem, vmem],
        out_specs=vmem,
        scratch_shapes=[
            pltpu.VMEM((3, node_count + GROUP, 128), jnp.float32),
            pltpu.SMEM((counts.shape[0] * (lists.shape[1] // BATCH) + TOGETHER,), jnp.int32),
        ],
        compiler_params=pltpu.CompilerParams(vmem_limit_bytes=40 * 1024 * 1024),
        name="volume",
    )(counts, lists, centres * scale, node_rows, coefs)
    return result[:node_count]


def per_device(struct_disp, target, inverse, centre_xyz, node_xyz):
    row_count = lax.axis_size("row")
    col_count = lax.axis_size("col")
    owner_count = row_count * col_count
    row_at = lax.axis_index("row")
    col_at = lax.axis_index("col")
    row_block, col_block = inverse.shape
    owner_block = row_block // col_count
    own_piece = row_block // col_count
    disp_rows, entries = struct_disp.shape

    slot_cap = max(2, 2 * entries // owner_count)
    owner_ids = target % col_block // owner_block * col_count + target // col_block
    offsets = target % owner_block
    at = jnp.arange(entries, dtype=jnp.int32)
    same = (owner_ids[:, None] == owner_ids[None, :]) & (at[:, None] < at[None, :])
    ranking = jnp.sum(same.astype(jnp.int32), axis=0)
    slot_ids = owner_ids * slot_cap + ranking
    pick = one_hot(slot_ids, 0, owner_count * slot_cap)
    outgoing = jnp.concatenate([struct_disp, offsets.astype(jnp.float32)[None, :] + 1.0], axis=0)
    sent = times_rows(pick, split_three(outgoing))
    width = disp_rows + 1
    sent = sent[:, :width] + sent[:, width : 2 * width] + sent[:, 2 * width :]
    received = lax.all_to_all(sent, ("row", "col"), split_axis=0, concat_axis=0, tiled=True)
    recv_offsets = received[:, disp_rows].astype(jnp.int32) - 1
    spots = one_hot(recv_offsets, 0, owner_block)
    centre_disp = join_three(times_rows(split_three(received[:, :disp_rows].T), spots))
    disp_bf = centre_disp.astype(jnp.bfloat16)
    disp_orders = (("z", "y"), ("y", "z"))
    disp_block = gather(disp_bf, row_count, col_count, disp_orders, (3, 1), False, 1)
    disp_block = disp_block.transpose(1, 0, 2).reshape(disp_rows, col_block)

    mine = lax.dynamic_slice_in_dim(centre_xyz, row_at * row_block, row_block, 1)
    order = one_hot(ranks(mine, CHUNK), col_at * own_piece, own_piece)
    placed_xyz = join_three(times_rows(split_three(mine), order))
    packed_xyz = placed_xyz.reshape(3 * own_piece // 128, 128)
    centres = gather(packed_xyz, row_count, col_count, (("z", "x", "y"),), (1,), True, 2)
    centres = centres.reshape(owner_count, 3, own_piece).transpose(1, 0, 2)
    centres = centres.reshape(3, centre_xyz.shape[1])
    node_order = one_hot(ranks(node_xyz, GROUP), 0, node_xyz.shape[1])
    nodes = join_three(times_rows(split_three(node_xyz), node_order))

    partial_value = times_rows(disp_block, inverse)
    coef_bf = lax.psum(partial_value, "col").astype(jnp.bfloat16)
    placed_coefs = times_rows(coef_bf, order).astype(jnp.bfloat16)
    coef_orders = (("x", "y", "z"), ("z", "x", "y"), ("z", "y", "x"))
    coefs = gather(placed_coefs, row_count, col_count, coef_orders, (2, 3, 3), True, 3)
    result = volume(coefs, centres, nodes)
    back = lax.dot_general(
        split_three(result.T), node_order, (((1,), (0,)), ((), ())), preferred_element_type=jnp.float32
    )
    return join_three(back)


def solution(mesh):
    placed = (
        P(None, ("row", "col")),
        P(("row", "col")),
        P("row", "col"),
        P(),
        P(None, ("row", "col")),
    )
    return jax.shard_map(
        per_device, mesh=mesh, in_specs=placed, out_specs=P(None, ("row", "col")), check_vma=False
    )
```
